32 devices in a mesh: depth: 4 (over y, x), probe: 8 (over z, core).
Axes of the slice: x: 2, y: 2, z: 4, core: 2. Of those that a mesh axis runs over, the one named last changes fastest.
Arguments:
- atom_blocks: bfloat16 [4, 1024, 128, 128], P('depth', 'probe'), may hold values from 0 to 1.5
- atom_tile: int32 [4, 1024], P('depth', 'probe'), may hold values from 0 to 255, as said below
- slice_counts: int32 [4], P('depth'), may hold values from 1 to 4, as said below
- positions: int32 [32], P('probe'), may hold values from 0 to 7, as said below
- probe_wave: float32 [2, 256, 256], replicated, may hold values from -4 to 4
- prop_phase: float32 [256, 256], replicated, may hold values from -3.140625 to 3.140625
Outputs:
- exit_waves: float32 [4, 32, 2, 256, 256], P('depth', 'probe')
The draws below stay inside these ranges and needn't reach their ends.
Inputs may be any that keep to these rules, and one draw needn't show every extreme that they name: `atom_tile`: tile number owner * 32 + s * 8 + c names tile row owner, slice slot s and tile column c, with s below slice_counts of that section. In each section the 128 atoms of one index of probe (aligned blocks) name at most 24 tiles of any one tile row, and in every draw each section has a tile row that receives exactly 24 from every such block. `slice_counts`: some section has exactly 4 slices in every draw. The 4 probes of one tile row (aligned blocks of 4) have distinct positions.
All inputs are finite; a program needn't handle non-finite values.
Results may differ from the reference program's by a relative error of at most 0.04.
Values may be sent and summed in bfloat16 or wider, within the bound.
A program may use at most 128 MiB of HBM per device.

```python
import math
import jax
import jax.numpy as jnp
from jax import lax

TILE = 128
SLICE_MAX = 4
TCOLS = 8
WAVES_DEV = 4
ATOMS_DEV = 128
N = 256
SECTIONS = 4
PROBES = 32
ATOMS = 1024
ROWS = 1024
COLS = 1024
TILES_DEV = 32
CAP = 24
N_PROBE = 8


def layout(key):
    draws = jax.random.randint(jax.random.fold_in(key, 101), (SECTIONS,), 1, SLICE_MAX + 1)
    full_at = jax.random.randint(jax.random.fold_in(key, 102), (), 0, SECTIONS)
    counts = draws.at[full_at].set(SLICE_MAX).astype(jnp.int32)
    owners = ATOMS // ATOMS_DEV
    hot_owner = jax.random.randint(jax.random.fold_in(key, 103), (SECTIONS,), 0, owners)
    remaining = ATOMS_DEV - CAP
    base_key = jax.random.fold_in(key, 104)

    def one_block(block_key, busy_owner, slice_limit):
        chosen = jax.random.permutation(jax.random.fold_in(block_key, 1), (owners - 1) * CAP)[:remaining]
        elsewhere = (chosen // CAP).astype(jnp.int32)
        elsewhere = elsewhere + (elsewhere >= busy_owner).astype(jnp.int32)
        owner_of = jnp.concatenate([jnp.full((CAP,), busy_owner, jnp.int32), elsewhere])
        owner_of = jax.random.permutation(jax.random.fold_in(block_key, 2), owner_of)
        slice_pick = jax.random.randint(jax.random.fold_in(block_key, 3), (ATOMS_DEV,), 0, slice_limit)
        col_pick = jax.random.randint(jax.random.fold_in(block_key, 4), (ATOMS_DEV,), 0, TCOLS)
        return (owner_of * TILES_DEV + slice_pick * TCOLS + col_pick).astype(jnp.int32)

    def one_section(section_index):

        def one_source(source_index):
            block_key = jax.random.fold_in(base_key, section_index * owners + source_index)
            return one_block(block_key, hot_owner[section_index], counts[section_index])
        return jax.vmap(one_source)(jnp.arange(owners, dtype=jnp.int32)).reshape(ATOMS)
    tiles = jax.vmap(one_section)(jnp.arange(SECTIONS, dtype=jnp.int32))
    return (counts, tiles.astype(jnp.int32))


def draw_slice_counts(key, part):
    return layout(key)[0]


def draw_atom_tile(key, part):
    return layout(key)[1]


def draw_positions(key, part):
    groups = PROBES // WAVES_DEV
    base_key = jax.random.fold_in(key, 200)

    def one_group(group_index):
        order = jax.random.permutation(jax.random.fold_in(base_key, group_index), jnp.arange(TCOLS, dtype=jnp.int32))
        return order[:WAVES_DEV]
    rows = jax.vmap(one_group)(jnp.arange(groups, dtype=jnp.int32))
    middle = 1 + jax.random.permutation(jax.random.fold_in(key, 300), jnp.arange(TCOLS - 2, dtype=jnp.int32))
    head = jnp.concatenate([jnp.array([0, TCOLS - 1], jnp.int32), middle])[:WAVES_DEV]
    head = jax.random.permutation(jax.random.fold_in(key, 301), head)
    rows = rows.at[0].set(head)
    return rows.reshape(PROBES).astype(jnp.int32)


def block_levels(rng, dims, cuts, smallest, largest):
    gain, own = 1.0, jax.random.fold_in(rng, 6)
    for dim, parts in cuts:
        steps = jnp.exp(jax.random.uniform(jax.random.fold_in(own, dim), (parts,), jnp.float32, smallest / len(cuts), largest / len(cuts)))
        gain = gain * jnp.repeat(steps, dims[dim] // parts).reshape([-1 if axis == dim else 1 for axis in range(len(dims))])
    return gain


def scatter_about(rng, dims, width, limit, held_as=jnp.bfloat16):
    values = width * jax.random.normal(rng, dims, jnp.float32)
    return jnp.clip(values, min=-limit, max=limit).astype(held_as)


def setup_inputs(seed: int = 0) -> dict:
    splits = jax.random.split(jax.random.key(seed), 7)
    atom_blocks = jnp.clip(1.5 * jax.random.uniform(splits[0], (SECTIONS, ATOMS, TILE, TILE), jnp.float32) ** block_levels(splits[0], (SECTIONS, ATOMS, TILE, TILE), ((0, 4), (1, 8)), -0.2, 0.2), 0.0, 1.5).astype(jnp.bfloat16)
    atom_tile = draw_atom_tile(jax.random.fold_in(splits[6], 71), 0)
    slice_counts = draw_slice_counts(jax.random.fold_in(splits[6], 71), 0)
    positions = draw_positions(jax.random.fold_in(splits[6], 71), 0)
    probe_wave = scatter_about(splits[4], (2, N, N), 0.5, 4.0, jnp.float32)
    prop_phase = jnp.clip(jax.random.uniform(splits[5], (N, N), jnp.float32, -3.140625, 3.140625), -3.140625, 3.140625)
    return dict(atom_blocks=atom_blocks, atom_tile=atom_tile, slice_counts=slice_counts, positions=positions, probe_wave=probe_wave, prop_phase=prop_phase)


SIGMA = 0.7

def dft_tables(points):
    grid_index = jnp.arange(points, dtype=jnp.int32)
    angle_table = (grid_index[:, None] * grid_index[None, :] % points).astype(jnp.float32) * (2.0 * math.pi / points)
    norm_scale = 1.0 / math.sqrt(points)
    real_part = (jnp.cos(angle_table) * norm_scale).astype(jnp.bfloat16)
    imag_part = (-jnp.sin(angle_table) * norm_scale).astype(jnp.bfloat16)
    return (real_part, imag_part)

def left_apply(real_part, imag_part, field):
    field = field.astype(jnp.float32)
    first_term = jnp.einsum('jk,bckl->bcjl', real_part.astype(jnp.float32), field, precision=lax.Precision.HIGHEST)
    second_term = jnp.einsum('jk,bckl->bcjl', imag_part.astype(jnp.float32), field, precision=lax.Precision.HIGHEST)
    return jnp.stack([first_term[:, 0] - second_term[:, 1], first_term[:, 1] + second_term[:, 0]], axis=1)

def right_apply(real_part, imag_part, field):
    field = field.astype(jnp.float32)
    first_term = jnp.einsum('bcjk,kl->bcjl', field, real_part.astype(jnp.float32), precision=lax.Precision.HIGHEST)
    second_term = jnp.einsum('bcjk,kl->bcjl', field, imag_part.astype(jnp.float32), precision=lax.Precision.HIGHEST)
    return jnp.stack([first_term[:, 0] - second_term[:, 1], first_term[:, 1] + second_term[:, 0]], axis=1)

def to_bf16(values):
    return lax.optimization_barrier(values.astype(jnp.bfloat16))

def slice_step(wave, cropped, real_part, imag_part, rotor_cos, rotor_sin):
    cosine = jnp.cos(SIGMA * cropped)
    sine_part = jnp.sin(SIGMA * cropped)
    wave_re = wave[:, 0]
    wave_im = wave[:, 1]
    passed = to_bf16(jnp.stack([wave_re * cosine - wave_im * sine_part, wave_re * sine_part + wave_im * cosine], axis=1))
    spectrum = to_bf16(left_apply(real_part, imag_part, passed))
    spectral = right_apply(real_part, imag_part, spectrum)
    propagated = to_bf16(jnp.stack([spectral[:, 0] * rotor_cos - spectral[:, 1] * rotor_sin, spectral[:, 0] * rotor_sin + spectral[:, 1] * rotor_cos], axis=1))
    returned = to_bf16(left_apply(real_part, -imag_part, propagated))
    return right_apply(real_part, -imag_part, returned)

def reference(atom_blocks, atom_tile, slice_counts, positions, probe_wave, prop_phase):
    real_part, imag_part = dft_tables(N)
    rotor_cos = jnp.cos(prop_phase)
    rotor_sin = jnp.sin(prop_phase)
    grid_index = jnp.arange(N, dtype=jnp.int32)
    groups = jnp.arange(PROBES, dtype=jnp.int32) // WAVES_DEV
    row_index = (groups[:, None] * TILE - TILE // 2 + grid_index[None, :]) % ROWS
    col_index = (positions[:, None].astype(jnp.int32) * TILE + grid_index[None, :]) % COLS
    wave = jnp.broadcast_to(probe_wave[None], (PROBES, 2, N, N)).astype(jnp.float32)
    collected = []
    for section in range(SECTIONS):
        flat = atom_blocks[section].astype(jnp.float32).reshape(ATOMS, TILE * TILE)
        summed = jax.ops.segment_sum(flat, atom_tile[section], num_segments=N_PROBE * TILES_DEV)
        field = summed.reshape(N_PROBE, SLICE_MAX, TCOLS, TILE, TILE).transpose(1, 0, 3, 2, 4).reshape(SLICE_MAX, ROWS, COLS)

        def one_slice(slice_index, current, field=field):
            plane = lax.dynamic_index_in_dim(field, slice_index, 0, keepdims=False)
            cropped = plane[row_index[:, :, None], col_index[:, None, :]]
            return slice_step(current, cropped, real_part, imag_part, rotor_cos, rotor_sin)
        wave = lax.fori_loop(0, slice_counts[section], one_slice, wave)
        collected.append(wave)
    return jnp.stack(collected, axis=0)
```

```python
import math

import jax
import jax.numpy as jnp
from jax import lax
from jax.sharding import PartitionSpec as P

SLICE_MAX = 4
TCOLS = 8


SIGMA = 0.7


def extended_2(x, sides, width):
    for axis, dim in sides:
        devices, length = (lax.axis_size(axis), x.shape[dim])
        up = [(i, (i + 1) % devices) for i in range(devices)]
        down = [(j, i) for i, j in up]
        last = lax.slice_in_dim(x, length - width, length, axis=dim)
        first = lax.slice_in_dim(x, 0, width, axis=dim)
        before = lax.ppermute(last, axis, up)
        after = lax.ppermute(first, axis, down)
        x = jnp.concatenate([before, x, after], axis=dim)
    return x


def shifted(block, axis, distance):
    devices = range(lax.axis_size(axis))
    route = [(i - distance, i) for i in devices if i - distance in devices]
    return lax.ppermute(block, axis, route)


def dft_tables(points):
    grid_index = jnp.arange(points, dtype=jnp.int32)
    angle_table = (grid_index[:, None] * grid_index[None, :] % points).astype(jnp.float32) * (
        2.0 * math.pi / points
    )
    norm_scale = 1.0 / math.sqrt(points)
    real_part = (jnp.cos(angle_table) * norm_scale).astype(jnp.bfloat16)
    imag_part = (-jnp.sin(angle_table) * norm_scale).astype(jnp.bfloat16)
    return (real_part, imag_part)


def left_apply(real_part, imag_part, field):
    first_term = jnp.einsum("jk,bckl->bcjl", real_part, field, preferred_element_type=jnp.float32)
    second_term = jnp.einsum("jk,bckl->bcjl", imag_part, field, preferred_element_type=jnp.float32)
    return jnp.stack(
        [first_term[:, 0] - second_term[:, 1], first_term[:, 1] + second_term[:, 0]], axis=1
    )


def right_apply(real_part, imag_part, field):
    first_term = jnp.einsum("bcjk,kl->bcjl", field, real_part, preferred_element_type=jnp.float32)
    second_term = jnp.einsum("bcjk,kl->bcjl", field, imag_part, preferred_element_type=jnp.float32)
    return jnp.stack(
        [first_term[:, 0] - second_term[:, 1], first_term[:, 1] + second_term[:, 0]], axis=1
    )


def slice_step(wave, cropped, real_part, imag_part, rotor_cos, rotor_sin):
    cosine = jnp.cos(SIGMA * cropped)
    sine_part = jnp.sin(SIGMA * cropped)
    wave_re = wave[:, 0]
    wave_im = wave[:, 1]
    passed = jnp.stack(
        [wave_re * cosine - wave_im * sine_part, wave_re * sine_part + wave_im * cosine], axis=1
    ).astype(jnp.bfloat16)
    spectrum = left_apply(real_part, imag_part, passed).astype(jnp.bfloat16)
    spectral = right_apply(real_part, imag_part, spectrum)
    propagated = jnp.stack(
        [
            spectral[:, 0] * rotor_cos - spectral[:, 1] * rotor_sin,
            spectral[:, 0] * rotor_sin + spectral[:, 1] * rotor_cos,
        ],
        axis=1,
    ).astype(jnp.bfloat16)
    returned = left_apply(real_part, -imag_part, propagated).astype(jnp.bfloat16)
    return right_apply(real_part, -imag_part, returned)


def assemble(blocks, slot_tiles, tiles_dev, tile_cols):
    slot_count, height, tile_size = blocks.shape
    member = (slot_tiles[:, None] == jnp.arange(tiles_dev, dtype=jnp.int32)[None, :]).astype(
        jnp.bfloat16
    )
    summed = jnp.einsum(
        "st,sk->tk",
        member,
        blocks.reshape(slot_count, height * tile_size),
        preferred_element_type=jnp.float32,
    )
    summed = summed.reshape(tiles_dev // tile_cols, tile_cols, height, tile_size)
    return summed.transpose(0, 2, 1, 3).reshape(
        tiles_dev // tile_cols, height, tile_cols * tile_size
    )


def shards(atom_blocks, atom_tile, slice_counts, positions, probe_wave, prop_phase):
    owners = lax.axis_size("probe")
    sections = lax.axis_size("depth")
    depth_index = lax.axis_index("depth")
    tile_size = atom_blocks.shape[-1]
    half_tile = tile_size // 2
    window = 2 * tile_size
    atoms_dev = atom_blocks.shape[1]
    capacity = max(2, 3 * atoms_dev // (2 * owners))
    tiles_dev = SLICE_MAX * TCOLS
    blocks = atom_blocks[0]
    targets = atom_tile[0]
    owner_of = targets // tiles_dev
    local_tile = targets % tiles_dev
    atom_index = jnp.arange(atoms_dev, dtype=jnp.int32)
    earlier = (owner_of[:, None] == owner_of[None, :]) & (atom_index[:, None] > atom_index[None, :])
    group_rank = jnp.sum(earlier.astype(jnp.int32), axis=1)
    slot_own = owner_of * capacity + group_rank
    empty_ids = jnp.full((owners * capacity,), -1, jnp.int32)
    outgoing = (
        jnp.zeros((owners * capacity, tile_size, tile_size), jnp.bfloat16).at[slot_own].set(blocks)
    )
    own_ids = empty_ids.at[slot_own].set(local_tile)
    arrived, arrived_tiles = (
        lax.all_to_all(outgoing, "probe", split_axis=0, concat_axis=0, tiled=True),
        lax.all_to_all(own_ids, "probe", split_axis=0, concat_axis=0, tiled=True),
    )
    stripe = assemble(arrived, arrived_tiles, tiles_dev, TCOLS)
    extended = extended_2(stripe, (("probe", 1),), half_tile)
    wrapped = jnp.concatenate([extended, extended[:, :, :tile_size]], axis=2)
    real_part, imag_part = dft_tables(window)
    rotor_cos = jnp.cos(prop_phase)
    rotor_sin = jnp.sin(prop_phase)
    slice_count = slice_counts[0]
    waves_dev = positions.shape[0]
    per_batch = 1
    batches = waves_dev // per_batch

    def crop_all(slice_index, offsets):
        plane = lax.dynamic_index_in_dim(wrapped, slice_index, 0, keepdims=False)

        def crop_one(offset):
            return lax.dynamic_slice(plane, (jnp.int32(0), offset * tile_size), (window, window))

        return jax.vmap(crop_one)(offsets)

    def run_section(entering, offsets):

        def one_slice(slice_index, wave):
            return slice_step(
                wave, crop_all(slice_index, offsets), real_part, imag_part, rotor_cos, rotor_sin
            )

        return lax.fori_loop(0, slice_count, one_slice, entering)

    def skip_section(entering, offsets):
        return entering

    launched = probe_wave[None]
    carried = jnp.zeros_like(launched)
    results = jnp.zeros((waves_dev, 2, window, window), jnp.float32)
    step_total = batches + sections - 1
    for step_index in range(step_total):
        micro_index = step_index - depth_index
        active = (micro_index >= 0) & (micro_index < batches)
        batch_start = jnp.clip(micro_index, 0, batches - 1) * per_batch
        offsets = lax.dynamic_slice_in_dim(positions, batch_start, per_batch)
        entering = jnp.where(depth_index == 0, launched, carried)
        leaving = lax.cond(active, run_section, skip_section, entering, offsets)
        updated = lax.dynamic_update_slice_in_dim(results, leaving, batch_start, 0)
        results = jnp.where(active, updated, results)
        if step_index + 1 < step_total:
            carried = shifted(leaving, "depth", 1)
    return results[None]


def solution(mesh):
    in_specs = (
        P("depth", "probe", None, None),
        P("depth", "probe"),
        P("depth"),
        P("probe"),
        P(),
        P(),
    )
    out_specs = P("depth", "probe", None, None, None)
    return jax.shard_map(shards, mesh=mesh, in_specs=in_specs, out_specs=out_specs, check_vma=False)
```

```python
import functools
import math

import jax
import jax.numpy as jnp
from jax import lax
from jax.experimental import pallas as pl
from jax.experimental.pallas import tpu as pltpu
from jax.sharding import PartitionSpec as P

SLICE_MAX = 4
TCOLS = 8


SIGMA = 0.7
PERIOD = 2.0 * math.pi / SIGMA
VMEM_LIMIT = 48 * 1024 * 1024


def reduced(value):
    return value - PERIOD * jnp.round(value * (1.0 / PERIOD))


def dft_tables(points):
    grid_index = jnp.arange(points, dtype=jnp.int32)
    angle_table = (grid_index[:, None] * grid_index[None, :] % points).astype(jnp.float32) * (
        2.0 * math.pi / points
    )
    norm_scale = 1.0 / math.sqrt(points)
    real_part = (jnp.cos(angle_table) * norm_scale).astype(jnp.bfloat16)
    imag_part = (-jnp.sin(angle_table) * norm_scale).astype(jnp.bfloat16)
    return (real_part, imag_part)


def rotor(phase):
    half = 0.5 * phase
    sq = half * half
    sine = half * (
        1.0
        + sq * (-1.0 / 6 + sq * (1.0 / 120 + sq * (-1.0 / 5040 + sq * (1.0 / 362880 - sq / 39916800.0))))
    )
    cosine = 1.0 + sq * (
        -0.5
        + sq
        * (1.0 / 24 + sq * (-1.0 / 720 + sq * (1.0 / 40320 + sq * (-1.0 / 3628800 + sq / 479001600.0))))
    )
    return 1.0 - 2.0 * sine * sine, 2.0 * sine * cosine


def sum_kernel(dests, tiles_dev, where_ref, mine_ref, own_ref, other_ref, kept_ref, sent_ref, total):
    total[...] = jnp.zeros_like(total)
    count = own_ref.shape[0]

    def add_from(ref, base):
        def body(atom, carry):
            place = where_ref[base + atom]

            @pl.when(place >= 0)
            def _():
                total[place] = total[place] + ref[atom].astype(jnp.float32)

            return carry

        lax.fori_loop(0, count, body, 0)

    add_from(own_ref, 0)
    add_from(other_ref, count)
    first = mine_ref[0] * tiles_dev

    def store_kept(tile, carry):
        kept_ref[tile] = total[first + tile]
        return carry

    lax.fori_loop(0, tiles_dev, store_kept, 0)

    def store_sent(tile, carry):
        sent_ref[tile] = reduced(total[tile]).astype(jnp.bfloat16)
        return carry

    lax.fori_loop(0, dests * tiles_dev, store_sent, 0)


def summed_atoms(where, mine, own, other, dests, tiles_dev):
    tile_size = own.shape[-1]
    rows = tile_size // 4
    smem = pl.BlockSpec(memory_space=pltpu.SMEM)

    def part(array_count):
        return pl.BlockSpec((array_count, rows, tile_size), lambda i: (0, i, 0))

    return pl.pallas_call(
        functools.partial(sum_kernel, dests, tiles_dev),
        grid=(tile_size // rows,),
        out_shape=(
            jax.ShapeDtypeStruct((tiles_dev, tile_size, tile_size), jnp.float32),
            jax.ShapeDtypeStruct((dests * tiles_dev, tile_size, tile_size), jnp.bfloat16),
        ),
        in_specs=[smem, smem, part(own.shape[0]), part(other.shape[0])],
        out_specs=(part(tiles_dev), part(dests * tiles_dev)),
        scratch_shapes=[pltpu.VMEM((dests * tiles_dev, rows, tile_size), jnp.float32)],
        compiler_params=pltpu.CompilerParams(vmem_limit_bytes=VMEM_LIMIT),
    )(where, mine, own, other)


def section_kernel(
    info,
    launched,
    carried,
    mid_a,
    mid_b,
    above_a,
    above_b,
    below_a,
    below_b,
    left,
    left_conj,
    right,
    right_conj,
    turn,
    former,
    result,
    leaving,
    wave,
):
    points = launched.shape[-1]
    active = info[0] > 0

    @pl.when(active)
    def _():
        @pl.when(info[1] > 0)
        def _():
            wave[...] = launched[...].reshape(2 * points, points)

        @pl.when(info[1] <= 0)
        def _():
            wave[...] = carried[...].reshape(2 * points, points).astype(jnp.float32)

        def right_apply(field, table):
            product = jnp.dot(field, table, preferred_element_type=jnp.float32)
            return (
                product[:points, :points] - product[points:, points:],
                product[:points, points:] + product[points:, :points],
            )

        def one_slice(s, carry):
            columns = [
                jnp.concatenate(
                    [above[s, 0].astype(jnp.float32), mid[s, 0], below[s, 0].astype(jnp.float32)],
                    axis=0,
                )
                for above, mid, below in ((above_a, mid_a, below_a), (above_b, mid_b, below_b))
            ]
            cosine, sine = rotor(SIGMA * jnp.concatenate(columns, axis=1))
            wave_re, wave_im = wave[:points], wave[points:]
            passed = jnp.concatenate(
                [wave_re * cosine - wave_im * sine, wave_re * sine + wave_im * cosine], axis=0
            ).astype(jnp.bfloat16)
            spectrum = jnp.dot(left[...], passed, preferred_element_type=jnp.float32)
            spec_re, spec_im = right_apply(spectrum.astype(jnp.bfloat16), right[...])
            turn_re, turn_im = turn[0], turn[1]
            propagated = jnp.concatenate(
                [spec_re * turn_re - spec_im * turn_im, spec_re * turn_im + spec_im * turn_re], axis=0
            ).astype(jnp.bfloat16)
            returned = jnp.dot(left_conj[...], propagated, preferred_element_type=jnp.float32)
            back_re, back_im = right_apply(returned.astype(jnp.bfloat16), right_conj[...])
            wave[:points] = back_re
            wave[points:] = back_im
            return carry

        lax.fori_loop(0, info[2], one_slice, 0)
        out = wave[...].reshape(2, points, points)
        result[0] = out
        leaving[...] = out.astype(jnp.bfloat16)

    @pl.when(jnp.logical_not(active))
    def _():
        result[...] = former[...]
        leaving[...] = jnp.zeros_like(leaving)


def run_section(info, launched, carried, mid, above, below, tables, results):
    points = launched.shape[-1]
    slots, _, tile_size, _ = mid.shape
    half = above.shape[2]

    def whole(array):
        return pl.BlockSpec(array.shape, lambda i, info, n=array.ndim: (0,) * n)

    def column(rows, which):
        return pl.BlockSpec((slots, 1, rows, tile_size), lambda i, info: (0, info[which], 0, 0))

    place = pl.BlockSpec((1, 2, points, points), lambda i, info: (info[5], 0, 0, 0))
    grid_spec = pltpu.PrefetchScalarGridSpec(
        num_scalar_prefetch=1,
        grid=(1,),
        in_specs=[
            whole(launched),
            whole(carried),
            column(tile_size, 3),
            column(tile_size, 4),
            column(half, 3),
            column(half, 4),
            column(half, 3),
            column(half, 4),
            *[whole(t) for t in tables],
            place,
        ],
        out_specs=[place, whole(carried)],
        scratch_shapes=[pltpu.VMEM((2 * points, points), jnp.float32)],
    )
    return pl.pallas_call(
        section_kernel,
        grid_spec=grid_spec,
        out_shape=[
            jax.ShapeDtypeStruct(results.shape, results.dtype),
            jax.ShapeDtypeStruct(carried.shape, carried.dtype),
        ],
        input_output_aliases={9 + len(tables): 0},
        compiler_params=pltpu.CompilerParams(vmem_limit_bytes=VMEM_LIMIT),
    )(info, launched, carried, mid, mid, above, above, below, below, *tables, results)


def shards(atom_blocks, atom_tile, slice_counts, positions, probe_wave, prop_phase):
    owners = lax.axis_size("probe")
    sections = lax.axis_size("depth")
    depth_index = lax.axis_index("depth")
    probe_index = lax.axis_index("probe")
    tile_size = atom_blocks.shape[-1]
    half_tile = tile_size // 2
    tiles_dev = SLICE_MAX * TCOLS
    pairs = owners // 2
    rank, core = probe_index // 2, probe_index % 2

    blocks, targets = atom_blocks[0], atom_tile[0]
    swap = [(i, i ^ 1) for i in range(owners)]
    other_blocks = lax.ppermute(blocks, "probe", swap)
    other_targets = lax.ppermute(targets, "probe", swap)
    named = jnp.concatenate([targets, other_targets])
    owner_of = named // tiles_dev
    where = jnp.where(owner_of % 2 == core, (owner_of // 2) * tiles_dev + named % tiles_dev, -1)
    kept, sent = summed_atoms(where, rank[None], blocks, other_blocks, pairs, tiles_dev)
    sent = sent.reshape(pairs, tiles_dev, tile_size, tile_size)

    up_in = down_in = None
    for step in range(pairs - 1):
        up_to = jnp.clip(pairs - 1 - step + rank, 0, pairs - 1)
        down_to = jnp.clip(step - (pairs - 1) + rank, 0, pairs - 1)
        up_out = lax.dynamic_index_in_dim(sent, up_to, 0, keepdims=False)
        down_out = lax.dynamic_index_in_dim(sent, down_to, 0, keepdims=False)
        if step:
            up_out = reduced(up_out.astype(jnp.float32) + up_in.astype(jnp.float32))
            down_out = reduced(down_out.astype(jnp.float32) + down_in.astype(jnp.float32))
            up_out, down_out = up_out.astype(jnp.bfloat16), down_out.astype(jnp.bfloat16)
        up_route, down_route = [], []
        for z in range(min(step + 1, pairs - 1)):
            for c in range(2):
                up_route.append((2 * z + c, 2 * (z + 1) + c))
                down_route.append((2 * (pairs - 1 - z) + c, 2 * (pairs - 2 - z) + c))
        up_in = lax.ppermute(up_out, "probe", up_route)
        down_in = lax.ppermute(down_out, "probe", down_route)
    if up_in is not None:
        kept = kept + up_in.astype(jnp.float32) + down_in.astype(jnp.float32)
    mid = reduced(kept).reshape(SLICE_MAX, TCOLS, tile_size, tile_size)
    narrow = mid.astype(jnp.bfloat16)
    up = [(i, (i + 1) % owners) for i in range(owners)]
    down = [(j, i) for i, j in up]
    above = lax.ppermute(narrow[:, :, half_tile:], "probe", up)
    below = lax.ppermute(narrow[:, :, :half_tile], "probe", down)

    real_part, imag_part = dft_tables(2 * tile_size)
    left = jnp.block([[real_part, -imag_part], [imag_part, real_part]])
    left_conj = jnp.block([[real_part, imag_part], [-imag_part, real_part]])
    right = jnp.concatenate([real_part, imag_part], axis=1)
    right_conj = jnp.concatenate([real_part, -imag_part], axis=1)
    turn = jnp.stack([jnp.cos(prop_phase), jnp.sin(prop_phase)])
    tables = (left, left_conj, right, right_conj, turn)

    waves_dev = positions.shape[0]
    results = jnp.zeros((waves_dev, *probe_wave.shape), jnp.float32)
    carried = jnp.zeros(probe_wave.shape, jnp.bfloat16)
    forward = [(d, d + 1) for d in range(sections - 1)]
    step_total = waves_dev + sections - 1
    for step in range(step_total):
        wave_index = step - depth_index
        active = (wave_index >= 0) & (wave_index < waves_dev)
        wave_index = jnp.clip(wave_index, 0, waves_dev - 1)
        column = positions[wave_index]
        info = jnp.stack(
            [
                active.astype(jnp.int32),
                (depth_index == 0).astype(jnp.int32),
                slice_counts[0],
                column,
                (column + 1) % TCOLS,
                wave_index,
            ]
        )
        results, leaving = run_section(
            info, probe_wave, carried, mid, above, below, tables, results
        )
        if step + 1 < step_total:
            carried = lax.ppermute(leaving, "depth", forward)
    return results[None]


def solution(mesh):
    in_specs = (
        P("depth", "probe", None, None),
        P("depth", "probe"),
        P("depth"),
        P("probe"),
        P(),
        P(),
    )
    out_specs = P("depth", "probe", None, None, None)
    return jax.shard_map(shards, mesh=mesh, in_specs=in_specs, out_specs=out_specs, check_vma=False)
```

```python
import functools
import math

import jax
import jax.numpy as jnp
from jax import lax
from jax.experimental import pallas as pl
from jax.experimental.pallas import tpu as pltpu
from jax.sharding import PartitionSpec as P

SLICE_MAX = 4
TCOLS = 8


SIGMA = 0.7
PERIOD = 2.0 * math.pi / SIGMA
VMEM_LIMIT = 48 * 1024 * 1024


def reduced(value):
    return value - PERIOD * jnp.round(value * (1.0 / PERIOD))


def dft_tables(points):
    grid_index = jnp.arange(points, dtype=jnp.int32)
    angle_table = (grid_index[:, None] * grid_index[None, :] % points).astype(jnp.float32) * (
        2.0 * math.pi / points
    )
    norm_scale = 1.0 / math.sqrt(points)
    real_part = (jnp.cos(angle_table) * norm_scale).astype(jnp.bfloat16)
    imag_part = (-jnp.sin(angle_table) * norm_scale).astype(jnp.bfloat16)
    return (real_part, imag_part)


def rotor(phase):
    half = 0.5 * phase
    sq = half * half
    sine = half * (
        1.0
        + sq * (-1.0 / 6 + sq * (1.0 / 120 + sq * (-1.0 / 5040 + sq * (1.0 / 362880 - sq / 39916800.0))))
    )
    cosine = 1.0 + sq * (
        -0.5
        + sq
        * (1.0 / 24 + sq * (-1.0 / 720 + sq * (1.0 / 40320 + sq * (-1.0 / 3628800 + sq / 479001600.0))))
    )
    return 1.0 - 2.0 * sine * sine, 2.0 * sine * cosine


def sum_kernel(dests, tiles_dev, plan_ref, mine_ref, own_ref, other_ref, kept_ref, sent_ref, total):
    total[...] = jnp.zeros_like(total)
    def add_from(ref, source):
        def body(entry, carry):
            place = plan_ref[source, 1, entry]
            total[place] = total[place] + ref[plan_ref[source, 0, entry]].astype(jnp.float32)
            return carry

        lax.fori_loop(0, mine_ref[1 + source], body, 0)

    add_from(own_ref, 0)
    add_from(other_ref, 1)
    first = mine_ref[0] * tiles_dev

    def store_kept(tile, carry):
        kept_ref[tile] = total[first + tile]
        return carry

    lax.fori_loop(0, tiles_dev, store_kept, 0)

    def store_sent(tile, carry):
        sent_ref[tile] = reduced(total[tile]).astype(jnp.bfloat16)
        return carry

    lax.fori_loop(0, dests * tiles_dev, store_sent, 0)


def summed_atoms(plan, mine, own, other, dests, tiles_dev):
    tile_size = own.shape[-1]
    rows = tile_size // 2
    smem = pl.BlockSpec(memory_space=pltpu.SMEM)

    def part(array_count):
        return pl.BlockSpec((array_count, rows, tile_size), lambda i: (0, i, 0))

    return pl.pallas_call(
        functools.partial(sum_kernel, dests, tiles_dev),
        grid=(tile_size // rows,),
        out_shape=(
            jax.ShapeDtypeStruct((tiles_dev, tile_size, tile_size), jnp.float32),
            jax.ShapeDtypeStruct((dests * tiles_dev, tile_size, tile_size), jnp.bfloat16),
        ),
        in_specs=[smem, smem, part(own.shape[0]), part(other.shape[0])],
        out_specs=(part(tiles_dev), part(dests * tiles_dev)),
        scratch_shapes=[pltpu.VMEM((dests * tiles_dev, rows, tile_size), jnp.float32)],
        compiler_params=pltpu.CompilerParams(vmem_limit_bytes=VMEM_LIMIT),
    )(plan, mine, own, other)


def section_kernel(
    step,
    info,
    launched,
    carried,
    mid_a,
    mid_b,
    above_a,
    above_b,
    below_a,
    below_b,
    left,
    left_conj,
    right,
    right_conj,
    turn,
    former,
    result,
    leaving,
    wave,
):
    points = launched.shape[-1]
    active = info[step, 0] > 0

    @pl.when(active)
    def _():
        @pl.when(info[step, 1] > 0)
        def _():
            wave[...] = launched[...].reshape(2 * points, points)

        @pl.when(info[step, 1] <= 0)
        def _():
            wave[...] = carried[...].reshape(2 * points, points).astype(jnp.float32)

        def right_apply(field, table):
            product = jnp.dot(field, table, preferred_element_type=jnp.float32)
            return (
                product[:points, :points] - product[points:, points:],
                product[:points, points:] + product[points:, :points],
            )

        def one_slice(s, carry):
            columns = [
                jnp.concatenate(
                    [above[s, 0].astype(jnp.float32), mid[s, 0], below[s, 0].astype(jnp.float32)],
                    axis=0,
                )
                for above, mid, below in ((above_a, mid_a, below_a), (above_b, mid_b, below_b))
            ]
            cosine, sine = rotor(SIGMA * jnp.concatenate(columns, axis=1))
            wave_re, wave_im = wave[:points], wave[points:]
            passed = jnp.concatenate(
                [wave_re * cosine - wave_im * sine, wave_re * sine + wave_im * cosine], axis=0
            ).astype(jnp.bfloat16)
            spectrum = jnp.dot(left[...], passed, preferred_element_type=jnp.float32)
            spec_re, spec_im = right_apply(spectrum.astype(jnp.bfloat16), right[...])
            turn_re, turn_im = turn[0], turn[1]
            propagated = jnp.concatenate(
                [spec_re * turn_re - spec_im * turn_im, spec_re * turn_im + spec_im * turn_re], axis=0
            ).astype(jnp.bfloat16)
            returned = jnp.dot(left_conj[...], propagated, preferred_element_type=jnp.float32)
            back_re, back_im = right_apply(returned.astype(jnp.bfloat16), right_conj[...])
            wave[:points] = back_re
            wave[points:] = back_im
            return carry

        lax.fori_loop(0, info[step, 2], one_slice, 0)
        out = wave[...].reshape(2, points, points)
        result[0] = out
        leaving[...] = out.astype(jnp.bfloat16)

    @pl.when(jnp.logical_not(active))
    def _():
        result[...] = former[...]
        leaving[...] = jnp.zeros_like(leaving)


def run_section(step, info, launched, carried, mid, above, below, tables, results):
    points = launched.shape[-1]
    slots, _, tile_size, _ = mid.shape
    half = above.shape[2]

    def whole(array):
        return pl.BlockSpec(array.shape, lambda i, info, n=array.ndim: (0,) * n)

    def column(rows, which):
        return pl.BlockSpec((slots, 1, rows, tile_size), lambda i, info: (0, info[step, which], 0, 0))

    place = pl.BlockSpec((1, 2, points, points), lambda i, info: (info[step, 5], 0, 0, 0))
    grid_spec = pltpu.PrefetchScalarGridSpec(
        num_scalar_prefetch=1,
        grid=(1,),
        in_specs=[
            whole(launched),
            whole(carried),
            column(tile_size, 3),
            column(tile_size, 4),
            column(half, 3),
            column(half, 4),
            column(half, 3),
            column(half, 4),
            *[whole(t) for t in tables],
            place,
        ],
        out_specs=[place, whole(carried)],
        scratch_shapes=[pltpu.VMEM((2 * points, points), jnp.float32)],
    )
    return pl.pallas_call(
        functools.partial(section_kernel, step),
        grid_spec=grid_spec,
        out_shape=[
            jax.ShapeDtypeStruct(results.shape, results.dtype),
            jax.ShapeDtypeStruct(carried.shape, carried.dtype),
        ],
        input_output_aliases={9 + len(tables): 0},
        compiler_params=pltpu.CompilerParams(vmem_limit_bytes=VMEM_LIMIT),
    )(info, launched, carried, mid, mid, above, above, below, below, *tables, results)


def shards(atom_blocks, atom_tile, slice_counts, positions, probe_wave, prop_phase):
    owners = lax.axis_size("probe")
    sections = lax.axis_size("depth")
    depth_index = lax.axis_index("depth")
    probe_index = lax.axis_index("probe")
    tile_size = atom_blocks.shape[-1]
    half_tile = tile_size // 2
    tiles_dev = SLICE_MAX * TCOLS
    pairs = owners // 2
    rank, core = probe_index // 2, probe_index % 2

    blocks, targets = atom_blocks[0], atom_tile[0]
    swap = [(i, i ^ 1) for i in range(owners)]
    other_blocks = lax.ppermute(blocks, "probe", swap)
    other_targets = lax.ppermute(targets, "probe", swap)
    named = jnp.stack([targets, other_targets])
    owner_of = named // tiles_dev
    counts = owner_of % 2 == core
    where = (owner_of // 2) * tiles_dev + named % tiles_dev
    atom = jnp.arange(named.shape[1], dtype=jnp.int32)
    earlier = counts[:, None, :] & (atom[None, :] < atom[:, None])[None]
    order = jnp.sum(earlier.astype(jnp.int32), axis=2)
    member = counts[:, None, :] & (order[:, None, :] == atom[None, :, None])
    entries = jnp.stack([jnp.broadcast_to(atom[None], named.shape), where], axis=1)
    plan = jnp.sum(jnp.where(member[:, None], entries[:, :, None, :], 0), axis=3)
    mine = jnp.concatenate([rank[None], jnp.sum(counts.astype(jnp.int32), axis=1)])
    kept, sent = summed_atoms(plan, mine, blocks, other_blocks, pairs, tiles_dev)
    sent = sent.reshape(pairs, tiles_dev, tile_size, tile_size)

    up_in = down_in = None
    for step in range(pairs - 1):
        up_to = jnp.clip(pairs - 1 - step + rank, 0, pairs - 1)
        down_to = jnp.clip(step - (pairs - 1) + rank, 0, pairs - 1)
        up_out = lax.dynamic_index_in_dim(sent, up_to, 0, keepdims=False)
        down_out = lax.dynamic_index_in_dim(sent, down_to, 0, keepdims=False)
        if step:
            up_out = reduced(up_out.astype(jnp.float32) + up_in.astype(jnp.float32))
            down_out = reduced(down_out.astype(jnp.float32) + down_in.astype(jnp.float32))
            up_out, down_out = up_out.astype(jnp.bfloat16), down_out.astype(jnp.bfloat16)
        up_route, down_route = [], []
        for z in range(min(step + 1, pairs - 1)):
            for c in range(2):
                up_route.append((2 * z + c, 2 * (z + 1) + c))
                down_route.append((2 * (pairs - 1 - z) + c, 2 * (pairs - 2 - z) + c))
        up_in = lax.ppermute(up_out, "probe", up_route)
        down_in = lax.ppermute(down_out, "probe", down_route)
        up_in, down_in = lax.optimization_barrier((up_in, down_in))
    if up_in is not None:
        kept = kept + up_in.astype(jnp.float32) + down_in.astype(jnp.float32)
    mid = reduced(kept).reshape(SLICE_MAX, TCOLS, tile_size, tile_size)
    narrow = mid.astype(jnp.bfloat16)
    up = [(i, (i + 1) % owners) for i in range(owners)]
    down = [(j, i) for i, j in up]
    above = lax.ppermute(narrow[:, :, half_tile:], "probe", up)
    below = lax.ppermute(narrow[:, :, :half_tile], "probe", down)

    real_part, imag_part = dft_tables(2 * tile_size)
    left = jnp.block([[real_part, -imag_part], [imag_part, real_part]])
    left_conj = jnp.block([[real_part, imag_part], [-imag_part, real_part]])
    right = jnp.concatenate([real_part, imag_part], axis=1)
    right_conj = jnp.concatenate([real_part, -imag_part], axis=1)
    turn = jnp.stack([jnp.cos(prop_phase), jnp.sin(prop_phase)])
    tables = (left, left_conj, right, right_conj, turn)

    waves_dev = positions.shape[0]
    results = jnp.zeros((waves_dev, *probe_wave.shape), jnp.float32)
    carried = jnp.zeros(probe_wave.shape, jnp.bfloat16)
    forward = [(d, d + 1) for d in range(sections - 1)]
    step_total = waves_dev + sections - 1
    wave_index = jnp.arange(step_total, dtype=jnp.int32) - depth_index
    active = (wave_index >= 0) & (wave_index < waves_dev)
    wave_index = jnp.clip(wave_index, 0, waves_dev - 1)
    chosen = wave_index[:, None] == jnp.arange(waves_dev, dtype=jnp.int32)[None, :]
    column = jnp.sum(jnp.where(chosen, positions[None, :], 0), axis=1)
    info = jnp.stack(
        [
            active.astype(jnp.int32),
            jnp.broadcast_to((depth_index == 0).astype(jnp.int32), active.shape),
            jnp.broadcast_to(slice_counts[0], active.shape),
            column,
            (column + 1) % TCOLS,
            wave_index,
        ],
        axis=1,
    )
    for step in range(step_total):
        results, leaving = run_section(
            step, info, probe_wave, carried, mid, above, below, tables, results
        )
        if step + 1 < step_total:
            carried = lax.ppermute(leaving, "depth", forward)
    return results[None]


def solution(mesh):
    in_specs = (
        P("depth", "probe", None, None),
        P("depth", "probe"),
        P("depth"),
        P("probe"),
        P(),
        P(),
    )
    out_specs = P("depth", "probe", None, None, None)
    return jax.shard_map(shards, mesh=mesh, in_specs=in_specs, out_specs=out_specs, check_vma=False)
```
